32 devices in a mesh: expert: 8 (over z, x), dp: 4 (over y, core).
Axes of the slice: x: 2, y: 2, z: 4, core: 2. Of those that a mesh axis runs over, the one named last changes fastest.
Arguments:
- tokens: bfloat16 [4096, 2048], P(('expert', 'dp')), may hold values from -6 to 6
- expert_index: int32 [4096, 4], P(('expert', 'dp')), may hold values from 0 to 7, all different within a row; in each aligned block of 128 rows (0 to 127, 128 to 255, ...) at most 96 rows name the same one
- gate_weights: bfloat16 [4096, 4], P(('expert', 'dp')), may hold values from 0.19921875 to 1
- w_gate: bfloat16 [8, 2048, 768], P('expert'), may hold values from -0.125 to 0.125
- w_up: bfloat16 [8, 2048, 768], P('expert'), may hold values from -0.125 to 0.125
- w_down: bfloat16 [8, 768, 2048], P('expert'), may hold values from -0.21875 to 0.21875
- v_gate: bfloat16 [8, 2048, 768], P('expert'), may hold values from -0.125 to 0.125
- v_up: bfloat16 [8, 2048, 768], P('expert'), may hold values from -0.125 to 0.125
- curvature: bfloat16 [2048, 2048], replicated, may hold values from -0.4 to 3.4, as said below
Outputs:
- hvp_gate: float32 [8, 768, 2048], P('expert', 'dp')
- hvp_up: float32 [8, 768, 2048], P('expert', 'dp')
- input_tangent: bfloat16 [4096, 2048], P(('expert', 'dp'))
The draws below stay inside these ranges and needn't reach their ends.
Inputs may be any that keep to these rules, and one draw needn't show every extreme that they name: `expert_index`: the 4 experts of a token differ. Among the rows of one device no expert is named more than 96 times, and in some device's rows one expert is named exactly 96 times. `curvature`: Symmetric.
All inputs are finite; a program needn't handle non-finite values.
Results may differ from the reference program's by a relative error of at most 0.014.
Values may be sent and summed in bfloat16 or wider, within the bound.
A program may use at most 128 MiB of HBM per device.

```python
import math
import jax
import jax.numpy as jnp
import numpy as np
from jax import lax

D = 2048
FF = 768
TOPK = 4
TOK_DEV = 128
EXPERTS = 8
CAP = 96
TOKENS = 4096
N_EXPERT = 8
N_DP = 4


def draw_curvature(key, part):
    base_key = jax.random.fold_in(key, 7)
    key_sym, key_diag = jax.random.split(base_key)
    normal_part = jax.random.normal(key_sym, (D, D), jnp.float32)
    symmetric = 0.45 * (normal_part + normal_part.T) / jnp.sqrt(2.0 * D)
    symmetric = jnp.clip(symmetric, -0.4, 0.4)
    diagonal = jnp.exp(jax.random.uniform(key_diag, (D,), jnp.float32, 0.0, jnp.log(2.5)))
    return (symmetric + jnp.diag(diagonal)).astype(jnp.bfloat16)


def levels(rng, dims, cuts, low, high):
    factor_of = 1.0
    for dim, parts in cuts:
        heights = jax.random.uniform(jax.random.fold_in(jax.random.fold_in(rng, 6), dim), (parts,), jnp.float32, low / len(cuts), high / len(cuts))
        factor_of = factor_of * jnp.repeat(jnp.exp(heights), dims[dim] // parts).reshape((-1,) + (1,) * (len(dims) - 1 - dim))
    return factor_of


def assign_block(key, own, number, rows, number_of, top, bound, lean):
    sequence = jax.random.permutation(key, number_of)
    heavy_load, usual = portions_of(number_of, rows * top, bound, lean, True), portions_of(number_of, rows * top, bound, lean, False)
    places = jnp.arange(number_of)

    def named(tallies, turn):
        used = int((tallies > 0).sum())
        fixed = max(1, used // 4)
        moved = fixed + (places - fixed + turn * (used - fixed)) % max(1, number_of - fixed)
        return jnp.zeros((number_of,), jnp.int32).at[sequence[jnp.where(places < fixed, places, moved)]].set(jnp.asarray(tallies, jnp.int32))

    tallies = jnp.where(number % 4 == 0, named(heavy_load, number // 4), named(usual, number - number // 4 - 1))
    mixed = jax.random.permutation(jax.random.fold_in(own, 3), number_of)
    donor, receiver = mixed[0:number_of // 2 * 2:2], mixed[1:number_of // 2 * 2:2]
    margin = jnp.minimum(tallies[donor] - 1, bound - tallies[receiver]) // 2
    margin = jnp.where((donor == sequence[0]) | (receiver == sequence[0]) | (tallies[receiver] == 0), 0, jnp.maximum(margin, 0))
    moved = jax.random.randint(jax.random.fold_in(own, 4), (number_of // 2,), 0, 1 << 20) % (margin + 1)
    tallies = tallies.at[donor].add(-moved).at[receiver].add(moved)
    members = jnp.searchsorted(jnp.cumsum(tallies), jnp.arange(rows * top), side="right").astype(jnp.int32)
    grid = members.reshape(top, rows).T
    grid = grid[jax.random.permutation(jax.random.fold_in(own, 1), rows)]
    turn = jax.random.randint(jax.random.fold_in(own, 2), (rows, 1), 0, top)
    return jnp.take_along_axis(grid, (jnp.arange(top)[None, :] + turn) % top, axis=1)


def portions_of(count, total, most, slope, full):
    loads = [(1 << 20) // math.isqrt(rank ** slope) + 1 for rank in range(1, count + 1)]
    largest = most if full else min(most, max(-(-total // count), total * loads[0] // sum(loads)))
    least = 1 if total - largest >= count - 1 else 0
    given, surplus = [largest] + [least] * (count - 1), total - largest - least * (count - 1)
    while surplus > 0:
        movable = [i for i in range(1, count) if given[i] < largest] or [i for i in range(1, count) if given[i] < most]
        whole, left = sum([loads[i] for i in movable]), surplus
        for i in movable:
            extra = min(most - given[i], max(1, left * loads[i] // whole), surplus)
            given[i] = given[i] + extra
            surplus = surplus - extra
    return np.array(given)


def bell_draw(key, dims, deviation, most, shards=(), held_as=jnp.bfloat16):
    result = jax.random.normal(key, dims, jnp.float32) * deviation
    if len(shards) > 0:
        result = levels(key, dims, shards, -0.22, 0.18) * result
    return jnp.clip(result, min=-most, max=most).astype(held_as)


def setup_inputs(seed: int = 0) -> dict:
    splits = jax.random.split(jax.random.key(seed), 10)
    tokens = bell_draw(splits[0], (TOKENS, D), 1.0, 6.0, ((0, 32),))
    expert_index_keys = jax.random.split(jax.random.fold_in(splits[1], 1), TOKENS // TOK_DEV)
    expert_index_turns = jax.random.permutation(jax.random.fold_in(splits[1], 3), TOKENS // TOK_DEV)
    expert_index = jax.vmap(lambda own, number: assign_block(jax.random.fold_in(splits[1], 2), own, number, TOK_DEV, EXPERTS, TOPK, CAP, 2))(expert_index_keys, expert_index_turns).reshape((TOKENS, TOPK))
    gate_weights = jnp.clip(0.19921875 + 0.80078125 * jax.random.uniform(splits[2], (TOKENS, TOPK), jnp.float32) ** levels(splits[2], (TOKENS, TOPK), ((0, 32),), -0.2, 0.2), 0.19921875, 1.0).astype(jnp.bfloat16)
    w_gate = bell_draw(splits[3], (EXPERTS, D, FF), D ** -0.5, 0.125, ((0, 8),))
    w_up = bell_draw(splits[4], (EXPERTS, D, FF), D ** -0.5, 0.125, ((0, 8),))
    w_down = bell_draw(splits[5], (EXPERTS, FF, D), FF ** -0.5, 0.21875, ((0, 8),))
    v_gate = bell_draw(splits[6], (EXPERTS, D, FF), D ** -0.5, 0.125, ((0, 8),))
    v_up = bell_draw(splits[7], (EXPERTS, D, FF), D ** -0.5, 0.125, ((0, 8),))
    curvature = draw_curvature(jax.random.fold_in(splits[9], 71), 0)
    return {"tokens": tokens, "expert_index": expert_index, "gate_weights": gate_weights, "w_gate": w_gate, "w_up": w_up, "w_down": w_down, "v_gate": v_gate, "v_up": v_up, "curvature": curvature}


def activation(gate_pre):
    sigmoid_val = jax.nn.sigmoid(gate_pre)
    return gate_pre * sigmoid_val, sigmoid_val * (1.0 + gate_pre * (1.0 - sigmoid_val))


def expert_rows(tokens, index_row, valid_row):
    picked = jnp.take(tokens, index_row, axis=0)
    return jnp.where(valid_row[:, None] > 0, picked, jnp.zeros_like(picked))


def group_sum(bar_rows, in_rows, group_cap, width):
    group_part = jnp.einsum("gri,grj->gij", bar_rows.reshape(N_DP, group_cap, width).astype(jnp.float32), in_rows.reshape(N_DP, group_cap, D).astype(jnp.float32))
    rounded = lax.optimization_barrier(group_part.astype(jnp.bfloat16))
    return jnp.sum(rounded.astype(jnp.float32), axis=0)


def reference(tokens, expert_index, gate_weights, w_gate, w_up, w_down, v_gate, v_up, curvature):
    routes_total = TOKENS * TOPK
    group_cap = N_EXPERT * CAP
    flat_ids = expert_index.reshape(-1).astype(jnp.int32)
    token_of = (jnp.arange(routes_total, dtype=jnp.int32) // TOPK).astype(jnp.int32)
    group_of = (token_of // TOK_DEV) % N_DP
    bucket = flat_ids * N_DP + group_of
    onehot = (bucket[:, None] == jnp.arange(EXPERTS * N_DP, dtype=jnp.int32)[None, :]).astype(jnp.int32)
    slot_rank = jnp.sum(jnp.cumsum(onehot, axis=0) * onehot, axis=1) - 1
    position = (bucket * group_cap + slot_rank).astype(jnp.int32)
    table_size = EXPERTS * N_DP * group_cap
    index_table = jnp.zeros((table_size,), jnp.int32).at[position].set(token_of).reshape(EXPERTS, -1)
    valid_table = jnp.zeros((table_size,), jnp.float32).at[position].set(1.0).reshape(EXPERTS, -1)
    gate_table = jnp.zeros((table_size,), jnp.float32).at[position].set(gate_weights.reshape(-1).astype(jnp.float32)).reshape(EXPERTS, -1)

    def first_pass(packed):
        index_row, valid_row, gate_row, w_gate_one, w_up_one, w_down_one, v_gate_one, v_up_one = packed
        in_rows = expert_rows(tokens, index_row, valid_row)
        gate_pre = jnp.dot(in_rows, w_gate_one, preferred_element_type=jnp.float32)
        up_pre = jnp.dot(in_rows, w_up_one, preferred_element_type=jnp.float32)
        gate_tan = jnp.dot(in_rows, v_gate_one, preferred_element_type=jnp.float32)
        up_tan = jnp.dot(in_rows, v_up_one, preferred_element_type=jnp.float32)
        silu_val, silu_slope = activation(gate_pre)
        hidden_tan = (silu_slope * up_pre * gate_tan + silu_val * up_tan).astype(jnp.bfloat16)
        return (gate_row[:, None] * jnp.dot(hidden_tan, w_down_one, preferred_element_type=jnp.float32)).astype(jnp.bfloat16)

    routed = lax.map(first_pass, (index_table, valid_table, gate_table, w_gate, w_up, w_down, v_gate, v_up)).reshape(table_size, D)
    route_pos = position.reshape(TOKENS, TOPK)
    token_sum = jnp.zeros((TOKENS, D), jnp.float32)
    for route_slot in range(TOPK):
        token_sum = token_sum + jnp.take(routed, route_pos[:, route_slot], axis=0).astype(jnp.float32)
    token_tan = token_sum.astype(jnp.bfloat16)
    curved = jnp.dot(token_tan, curvature, preferred_element_type=jnp.float32).astype(jnp.bfloat16)

    def second_pass(packed):
        index_row, valid_row, gate_row, w_gate_one, w_up_one, w_down_one = packed
        in_rows = expert_rows(tokens, index_row, valid_row)
        curved_rows = expert_rows(curved, index_row, valid_row)
        gate_pre = jnp.dot(in_rows, w_gate_one, preferred_element_type=jnp.float32)
        up_pre = jnp.dot(in_rows, w_up_one, preferred_element_type=jnp.float32)
        silu_val, silu_slope = activation(gate_pre)
        back_hidden = gate_row[:, None] * jnp.dot(curved_rows, w_down_one.T, preferred_element_type=jnp.float32)
        gate_bar = (back_hidden * up_pre * silu_slope).astype(jnp.bfloat16)
        up_bar = (back_hidden * silu_val).astype(jnp.bfloat16)
        hvp_gate_one = group_sum(gate_bar, in_rows, group_cap, FF)
        hvp_up_one = group_sum(up_bar, in_rows, group_cap, FF)
        route_in = jnp.dot(gate_bar, w_gate_one.T, preferred_element_type=jnp.float32) + jnp.dot(up_bar, w_up_one.T, preferred_element_type=jnp.float32)
        return hvp_gate_one, hvp_up_one, route_in.astype(jnp.bfloat16)

    hvp_gate, hvp_up, route_in = lax.map(second_pass, (index_table, valid_table, gate_table, w_gate, w_up, w_down))
    route_flat = route_in.reshape(table_size, D)
    input_sum = jnp.zeros((TOKENS, D), jnp.float32)
    for route_slot in range(TOPK):
        input_sum = input_sum + jnp.take(route_flat, route_pos[:, route_slot], axis=0).astype(jnp.float32)
    return hvp_gate, hvp_up, input_sum.astype(jnp.bfloat16)
```

```python
import functools

import jax
import jax.numpy as jnp
from jax import lax
from jax.experimental import pallas as pl
from jax.experimental.pallas import tpu as pltpu
from jax.sharding import PartitionSpec as P

BF = jnp.bfloat16
F32 = jnp.float32
MESH = pl.DeviceIdType.MESH


def dot(a, b, ca=1, cb=0):
    return lax.dot_general(a, b, (((ca,), (cb,)), ((), ())), preferred_element_type=F32)


def peers(nz, nx):
    me = lax.axis_index("expert")
    return me, lax.div(me, nx), lax.rem(me, nx)


def greet(nz, nx):
    me, z, x = peers(nz, nx)
    barrier = pltpu.get_barrier_semaphore()

    def hello(target):
        pl.semaphore_signal(barrier, inc=1, device_id={"expert": target}, device_id_type=MESH)

    for k in range(1, nx):
        hello(z * nx + lax.rem(x + k, nx))

    @pl.when(z < nz - 1)
    def _():
        hello(me + nx)

    @pl.when(z > 0)
    def _():
        hello(me - nx)

    ends = (z == 0).astype(jnp.int32) + (z == nz - 1).astype(jnp.int32)
    pl.semaphore_wait(barrier, nx + 1 - ends)


def remote(src, dst, send_sem, recv_sem, target):
    return pltpu.make_async_remote_copy(
        src_ref=src,
        dst_ref=dst,
        send_sem=send_sem,
        recv_sem=recv_sem,
        device_id={"expert": target},
        device_id_type=MESH,
    )


def gather_kernel(nz, nx, count, *refs):
    ins, outs = refs[:count], refs[count : 2 * count]
    own_sem, up_sem, down_sem, side_sem, recv_sem = refs[2 * count :]
    me, z, x = peers(nz, nx)
    greet(nz, nx)

    def up(i, src, zs):
        slot = zs * nx + x
        return remote(src, outs[i].at[slot], up_sem.at[i, zs], recv_sem.at[i, slot], me + nx)

    def down(i, src, zs):
        slot = zs * nx + x
        return remote(src, outs[i].at[slot], down_sem.at[i, zs], recv_sem.at[i, slot], me - nx)

    def side(i, src, zs, k):
        slot = zs * nx + x
        target = z * nx + lax.rem(x + k, nx)
        return remote(src, outs[i].at[slot], side_sem.at[i, zs, k], recv_sem.at[i, slot], target)

    def arrived(i, slot):
        here = outs[i].at[slot]
        remote(here, here, own_sem.at[i], recv_sem.at[i, slot], z * nx + lax.rem(x + 1, nx)).wait_recv()

    def copy_own(i):
        return pltpu.make_async_copy(ins[i], outs[i].at[me], own_sem.at[i])

    for i in range(count):
        for k in range(1, nx):
            side(i, ins[i], z, k).start()

        @pl.when(z < nz - 1)
        def _():
            up(i, ins[i], z).start()

        @pl.when(z > 0)
        def _():
            down(i, ins[i], z).start()

        copy_own(i).start()
    for d in range(1, nz):
        for i in range(count):

            @pl.when(z - d >= 0)
            def _():
                slot = (z - d) * nx + x
                arrived(i, slot)

                @pl.when(z < nz - 1)
                def _():
                    up(i, outs[i].at[slot], z - d).start()

                for k in range(1, nx):
                    side(i, outs[i].at[slot], z - d, k).start()

            @pl.when(z + d < nz)
            def _():
                slot = (z + d) * nx + x
                arrived(i, slot)

                @pl.when(z > 0)
                def _():
                    down(i, outs[i].at[slot], z + d).start()

                for k in range(1, nx):
                    side(i, outs[i].at[slot], z + d, k).start()

    for i in range(count):
        for zs in range(nz):
            slot = zs * nx + x
            for k in range(1, nx):
                arrived(i, zs * nx + lax.rem(x + k, nx))
                side(i, ins[i], zs, k).wait_send()

            @pl.when((z < nz - 1) & (zs <= z))
            def _():
                up(i, ins[i], zs).wait_send()

            @pl.when((z > 0) & (zs >= z))
            def _():
                down(i, ins[i], zs).wait_send()

        copy_own(i).wait()


def scatter_kernel(nz, nx, p_ref, out_ref, side_buf, up_buf, down_buf, stage, acc, side_send, side_recv, line_send, line_recv):
    me, z, x = peers(nz, nx)
    greet(nz, nx)

    def side(zd, k):
        peer = lax.rem(x + k, nx)
        return remote(
            p_ref.at[zd * nx + peer], side_buf.at[zd, k - 1], side_send.at[zd, k - 1],
            side_recv.at[zd, k - 1], z * nx + peer,
        )

    def up(zd):
        return remote(stage.at[zd], up_buf.at[zd], line_send.at[0, zd], line_recv.at[0, zd], me + nx)

    def down(zd):
        return remote(stage.at[zd], down_buf.at[zd], line_send.at[1, zd], line_recv.at[1, zd], me - nx)

    def begin(zd):
        for k in range(1, nx):
            side(zd, k).start()

    def total(zd):
        for k in range(1, nx):
            side(zd, k).wait_recv()
        value = p_ref[zd * nx + x].astype(F32)
        for k in range(1, nx):
            value = value + side_buf[zd, k - 1].astype(F32)
        acc[...] = value

    def from_below(zd):
        @pl.when(z > 0)
        def _():
            up(zd).wait_recv()
            acc[...] += up_buf[zd].astype(F32)

    def from_above(zd):
        @pl.when(z < nz - 1)
        def _():
            down(zd).wait_recv()
            acc[...] += down_buf[zd].astype(F32)

    for d in range(nz - 1, 0, -1):

        @pl.when(z + d < nz)
        def _():
            begin(z + d)

        @pl.when(z - d >= 0)
        def _():
            begin(z - d)

    begin(z)
    for d in range(nz - 1, 0, -1):

        @pl.when(z + d < nz)
        def _():
            total(z + d)
            from_below(z + d)
            stage[z + d] = acc[...].astype(BF)
            up(z + d).start()

        @pl.when(z - d >= 0)
        def _():
            total(z - d)
            from_above(z - d)
            stage[z - d] = acc[...].astype(BF)
            down(z - d).start()

    total(z)
    from_below(z)
    from_above(z)
    out_ref[...] = acc[...].astype(BF)
    for zd in range(nz):
        for k in range(1, nx):
            side(zd, k).wait_send()

        @pl.when(zd > z)
        def _():
            up(zd).wait_send()

        @pl.when(zd < z)
        def _():
            down(zd).wait_send()


def gather(nz, nx, number, *arrays):
    n, m = nz * nx, len(arrays)
    made = pl.pallas_call(
        functools.partial(gather_kernel, nz, nx, m),
        out_shape=[jax.ShapeDtypeStruct((n, *a.shape), a.dtype) for a in arrays],
        in_specs=[pl.BlockSpec(memory_space=pl.ANY)] * m,
        out_specs=[pl.BlockSpec(memory_space=pl.ANY)] * m,
        scratch_shapes=[
            pltpu.SemaphoreType.DMA((m,)),
            pltpu.SemaphoreType.DMA((m, nz)),
            pltpu.SemaphoreType.DMA((m, nz)),
            pltpu.SemaphoreType.DMA((m, nz, nx)),
            pltpu.SemaphoreType.DMA((m, n)),
        ],
        compiler_params=pltpu.CompilerParams(collective_id=number, has_side_effects=True),
    )(*arrays)
    return [a.reshape(-1, a.shape[-1]) for a in made]


def scatter(nz, nx, number, p):
    rows, width = p.shape[0] // (nz * nx), p.shape[1]
    block = (rows, width)
    return pl.pallas_call(
        functools.partial(scatter_kernel, nz, nx),
        out_shape=jax.ShapeDtypeStruct(block, BF),
        in_specs=[pl.BlockSpec(memory_space=pltpu.VMEM)],
        out_specs=pl.BlockSpec(memory_space=pltpu.VMEM),
        scratch_shapes=[
            pltpu.VMEM((nz, max(nx - 1, 1), *block), BF),
            pltpu.VMEM((nz, *block), BF),
            pltpu.VMEM((nz, *block), BF),
            pltpu.VMEM((nz, *block), BF),
            pltpu.VMEM(block, F32),
            pltpu.SemaphoreType.DMA((nz, max(nx - 1, 1))),
            pltpu.SemaphoreType.DMA((nz, max(nx - 1, 1))),
            pltpu.SemaphoreType.DMA((2, nz)),
            pltpu.SemaphoreType.DMA((2, nz)),
        ],
        compiler_params=pltpu.CompilerParams(
            collective_id=number, has_side_effects=True, vmem_limit_bytes=48 * 2**20
        ),
    )(p.reshape(nz * nx, *block))


def shards(
    nz, nx, tokens, expert_index, gate_weights, w_gate, w_up, w_down, v_gate, v_up, curvature
):
    experts = lax.axis_size("expert")
    mine = lax.axis_index("expert")
    chosen = expert_index[:, :, None] == jnp.arange(experts, dtype=jnp.int32)[None, None, :]
    gates = jnp.sum(jnp.where(chosen, gate_weights[:, :, None].astype(F32), 0.0), axis=1).astype(BF)
    pad = -experts % 128
    x, all_gates = gather(nz, nx, 0, tokens, jnp.pad(gates, ((0, 0), (0, pad))))
    column = jnp.arange(experts + pad, dtype=jnp.int32)[None, :] == mine
    g = jnp.sum(jnp.where(column, all_gates.astype(F32), 0.0), axis=1, keepdims=True)
    wg, wu, wd, vg, vu = w_gate[0], w_up[0], w_down[0], v_gate[0], v_up[0]
    gate_pre, up_pre, gate_tan, up_tan = dot(x, wg), dot(x, wu), dot(x, vg), dot(x, vu)
    s = jax.nn.sigmoid(gate_pre)
    silu = gate_pre * s
    slope = s * (1.0 + gate_pre * (1.0 - s))
    hidden = (slope * up_pre * gate_tan + silu * up_tan).astype(BF)
    token_tan = scatter(nz, nx, 1, (g * dot(hidden, wd)).astype(BF))
    curved = dot(token_tan, curvature).astype(BF)
    (c,) = gather(nz, nx, 2, curved)
    back = g * dot(c, wd, 1, 1)
    gate_bar = (back * up_pre * slope).astype(BF)
    up_bar = (back * silu).astype(BF)
    gate_term = dot(gate_bar, x, 0, 0).astype(BF)
    up_term = dot(up_bar, x, 0, 0).astype(BF)
    hvp_gate = lax.psum_scatter(gate_term[None], "dp", scatter_dimension=1, tiled=True).astype(F32)
    hvp_up = lax.psum_scatter(up_term[None], "dp", scatter_dimension=1, tiled=True).astype(F32)
    route_in = (dot(gate_bar, wg, 1, 1) + dot(up_bar, wu, 1, 1)).astype(BF)
    return hvp_gate, hvp_up, scatter(nz, nx, 3, route_in)


def solution(mesh):
    experts = mesh.shape["expert"]
    column = mesh.devices.reshape(experts, -1)[:, 0]
    nx = len({device.coords[0] for device in column})
    nx = nx if experts % nx == 0 else 1
    return jax.shard_map(
        functools.partial(shards, experts // nx, nx),
        mesh=mesh,
        in_specs=(
            P(("expert", "dp"), None),
            P(("expert", "dp"), None),
            P(("expert", "dp"), None),
            P("expert", None, None),
            P("expert", None, None),
            P("expert", None, None),
            P("expert", None, None),
            P("expert", None, None),
            P(),
        ),
        out_specs=(P("expert", "dp", None), P("expert", "dp", None), P(("expert", "dp"), None)),
        check_vma=False,
    )
```

```python
import functools

import jax
import jax.numpy as jnp
from jax import lax
from jax.experimental import pallas as pl
from jax.experimental.pallas import tpu as pltpu
from jax.sharding import PartitionSpec as P

BF = jnp.bfloat16
F32 = jnp.float32
MESH = pl.DeviceIdType.MESH


def dot(a, b, ca=1, cb=0):
    return lax.dot_general(a, b, (((ca,), (cb,)), ((), ())), preferred_element_type=F32)


def peers(nz, nx):
    me = lax.axis_index("expert")
    return me, lax.div(me, nx), lax.rem(me, nx)


def greet(nz, nx):
    me, z, x = peers(nz, nx)
    barrier = pltpu.get_barrier_semaphore()

    def hello(target):
        pl.semaphore_signal(barrier, inc=1, device_id={"expert": target}, device_id_type=MESH)

    for k in range(1, nx):
        hello(z * nx + lax.rem(x + k, nx))

    @pl.when(z < nz - 1)
    def _():
        hello(me + nx)

    @pl.when(z > 0)
    def _():
        hello(me - nx)

    ends = (z == 0).astype(jnp.int32) + (z == nz - 1).astype(jnp.int32)
    pl.semaphore_wait(barrier, nx + 1 - ends)


def remote(src, dst, send_sem, recv_sem, target):
    return pltpu.make_async_remote_copy(
        src_ref=src,
        dst_ref=dst,
        send_sem=send_sem,
        recv_sem=recv_sem,
        device_id={"expert": target},
        device_id_type=MESH,
    )


def gather_kernel(nz, nx, count, *refs):
    ins, outs = refs[:count], refs[count : 2 * count]
    own_sem, up_sem, down_sem, side_sem, recv_sem = refs[2 * count :]
    me, z, x = peers(nz, nx)
    greet(nz, nx)

    def up(i, src, zs):
        slot = zs * nx + x
        return remote(src, outs[i].at[slot], up_sem.at[i, zs], recv_sem.at[i, slot], me + nx)

    def down(i, src, zs):
        slot = zs * nx + x
        return remote(src, outs[i].at[slot], down_sem.at[i, zs], recv_sem.at[i, slot], me - nx)

    def side(i, src, zs, k):
        slot = zs * nx + x
        target = z * nx + lax.rem(x + k, nx)
        return remote(src, outs[i].at[slot], side_sem.at[i, zs, k], recv_sem.at[i, slot], target)

    def arrived(i, slot):
        here = outs[i].at[slot]
        remote(here, here, own_sem.at[i], recv_sem.at[i, slot], z * nx + lax.rem(x + 1, nx)).wait_recv()

    def copy_own(i):
        return pltpu.make_async_copy(ins[i], outs[i].at[me], own_sem.at[i])

    for i in range(count):
        for k in range(1, nx):
            side(i, ins[i], z, k).start()

        @pl.when(z < nz - 1)
        def _():
            up(i, ins[i], z).start()

        @pl.when(z > 0)
        def _():
            down(i, ins[i], z).start()

        copy_own(i).start()
    for d in range(1, nz):
        for i in range(count):

            @pl.when(z - d >= 0)
            def _():
                slot = (z - d) * nx + x
                arrived(i, slot)

                @pl.when(z < nz - 1)
                def _():
                    up(i, outs[i].at[slot], z - d).start()

                for k in range(1, nx):
                    side(i, outs[i].at[slot], z - d, k).start()

            @pl.when(z + d < nz)
            def _():
                slot = (z + d) * nx + x
                arrived(i, slot)

                @pl.when(z > 0)
                def _():
                    down(i, outs[i].at[slot], z + d).start()

                for k in range(1, nx):
                    side(i, outs[i].at[slot], z + d, k).start()

    for i in range(count):
        for zs in range(nz):
            slot = zs * nx + x
            for k in range(1, nx):
                arrived(i, zs * nx + lax.rem(x + k, nx))
                side(i, ins[i], zs, k).wait_send()

            @pl.when((z < nz - 1) & (zs <= z))
            def _():
                up(i, ins[i], zs).wait_send()

            @pl.when((z > 0) & (zs >= z))
            def _():
                down(i, ins[i], zs).wait_send()

        copy_own(i).wait()


def scatter_kernel(nz, nx, p_ref, out_ref, side_buf, up_buf, down_buf, stage, acc, side_send, side_recv, line_send, line_recv):
    me, z, x = peers(nz, nx)
    greet(nz, nx)

    def side(zd, k):
        peer = lax.rem(x + k, nx)
        return remote(
            p_ref.at[zd * nx + peer], side_buf.at[zd, k - 1], side_send.at[zd, k - 1],
            side_recv.at[zd, k - 1], z * nx + peer,
        )

    def up(zd):
        return remote(stage.at[zd], up_buf.at[zd], line_send.at[0, zd], line_recv.at[0, zd], me + nx)

    def down(zd):
        return remote(stage.at[zd], down_buf.at[zd], line_send.at[1, zd], line_recv.at[1, zd], me - nx)

    def begin(zd):
        for k in range(1, nx):
            side(zd, k).start()

    def total(zd):
        for k in range(1, nx):
            side(zd, k).wait_recv()
        value = p_ref[zd * nx + x].astype(F32)
        for k in range(1, nx):
            value = value + side_buf[zd, k - 1].astype(F32)
        acc[...] = value

    def from_below(zd):
        @pl.when(z > 0)
        def _():
            up(zd).wait_recv()
            acc[...] += up_buf[zd].astype(F32)

    def from_above(zd):
        @pl.when(z < nz - 1)
        def _():
            down(zd).wait_recv()
            acc[...] += down_buf[zd].astype(F32)

    for d in range(nz - 1, 0, -1):

        @pl.when(z + d < nz)
        def _():
            begin(z + d)

        @pl.when(z - d >= 0)
        def _():
            begin(z - d)

    begin(z)
    for d in range(nz - 1, 0, -1):

        @pl.when(z + d < nz)
        def _():
            total(z + d)
            from_below(z + d)
            stage[z + d] = acc[...].astype(BF)
            up(z + d).start()

        @pl.when(z - d >= 0)
        def _():
            total(z - d)
            from_above(z - d)
            stage[z - d] = acc[...].astype(BF)
            down(z - d).start()

    total(z)
    from_below(z)
    from_above(z)
    out_ref[...] = acc[...].astype(BF)
    for zd in range(nz):
        for k in range(1, nx):
            side(zd, k).wait_send()

        @pl.when(zd > z)
        def _():
            up(zd).wait_send()

        @pl.when(zd < z)
        def _():
            down(zd).wait_send()


def gather(nz, nx, number, *arrays):
    n, m = nz * nx, len(arrays)
    made = pl.pallas_call(
        functools.partial(gather_kernel, nz, nx, m),
        out_shape=[jax.ShapeDtypeStruct((n, *a.shape), a.dtype) for a in arrays],
        in_specs=[pl.BlockSpec(memory_space=pl.ANY)] * m,
        out_specs=[pl.BlockSpec(memory_space=pl.ANY)] * m,
        scratch_shapes=[
            pltpu.SemaphoreType.DMA((m,)),
            pltpu.SemaphoreType.DMA((m, nz)),
            pltpu.SemaphoreType.DMA((m, nz)),
            pltpu.SemaphoreType.DMA((m, nz, nx)),
            pltpu.SemaphoreType.DMA((m, n)),
        ],
        compiler_params=pltpu.CompilerParams(collective_id=number, has_side_effects=True),
    )(*arrays)
    return [a.reshape(-1, a.shape[-1]) for a in made]


def scatter(nz, nx, number, p):
    rows, width = p.shape[0] // (nz * nx), p.shape[1]
    block = (rows, width)
    return pl.pallas_call(
        functools.partial(scatter_kernel, nz, nx),
        out_shape=jax.ShapeDtypeStruct(block, BF),
        in_specs=[pl.BlockSpec(memory_space=pltpu.VMEM)],
        out_specs=pl.BlockSpec(memory_space=pltpu.VMEM),
        scratch_shapes=[
            pltpu.VMEM((nz, max(nx - 1, 1), *block), BF),
            pltpu.VMEM((nz, *block), BF),
            pltpu.VMEM((nz, *block), BF),
            pltpu.VMEM((nz, *block), BF),
            pltpu.VMEM(block, F32),
            pltpu.SemaphoreType.DMA((nz, max(nx - 1, 1))),
            pltpu.SemaphoreType.DMA((nz, max(nx - 1, 1))),
            pltpu.SemaphoreType.DMA((2, nz)),
            pltpu.SemaphoreType.DMA((2, nz)),
        ],
        compiler_params=pltpu.CompilerParams(
            collective_id=number, has_side_effects=True, vmem_limit_bytes=48 * 2**20
        ),
    )(p.reshape(nz * nx, *block))


def shards(
    nz, nx, tokens, expert_index, gate_weights, w_gate, w_up, w_down, v_gate, v_up, curvature
):
    experts = lax.axis_size("expert")
    mine = lax.axis_index("expert")
    chosen = expert_index[:, :, None] == jnp.arange(experts, dtype=jnp.int32)[None, None, :]
    gates = jnp.sum(jnp.where(chosen, gate_weights[:, :, None].astype(F32), 0.0), axis=1).astype(BF)
    gates = jnp.pad(gates.T, ((0, -experts % 16), (0, 0)))
    all_gates, x = gather(nz, nx, 0, gates, tokens)
    all_gates = all_gates.reshape(experts, *gates.shape).astype(F32)
    is_mine = jnp.arange(gates.shape[0], dtype=jnp.int32)[None, :, None] == mine
    g = jnp.sum(jnp.where(is_mine, all_gates, 0.0), axis=1).reshape(-1, 1)
    wg, wu, wd, vg, vu = w_gate[0], w_up[0], w_down[0], v_gate[0], v_up[0]
    gate_pre, up_pre, gate_tan, up_tan = dot(x, wg), dot(x, wu), dot(x, vg), dot(x, vu)
    s = jax.nn.sigmoid(gate_pre)
    silu = gate_pre * s
    slope = s * (1.0 + gate_pre * (1.0 - s))
    hidden = (slope * up_pre * gate_tan + silu * up_tan).astype(BF)
    token_tan = scatter(nz, nx, 1, (g * dot(hidden, wd)).astype(BF))
    curved = dot(token_tan, curvature).astype(BF)
    (c,) = gather(nz, nx, 2, curved)
    back = g * dot(c, wd, 1, 1)
    gate_bar = (back * up_pre * slope).astype(BF)
    up_bar = (back * silu).astype(BF)
    gate_term = dot(gate_bar, x, 0, 0).astype(BF)
    up_term = dot(up_bar, x, 0, 0).astype(BF)
    hvp_gate = lax.psum_scatter(gate_term[None], "dp", scatter_dimension=1, tiled=True).astype(F32)
    hvp_up = lax.psum_scatter(up_term[None], "dp", scatter_dimension=1, tiled=True).astype(F32)
    route_in = (dot(gate_bar, wg, 1, 1) + dot(up_bar, wu, 1, 1)).astype(BF)
    return hvp_gate, hvp_up, scatter(nz, nx, 3, route_in)


def solution(mesh):
    experts = mesh.shape["expert"]
    column = mesh.devices.reshape(experts, -1)[:, 0]
    nx = len({device.coords[0] for device in column})
    nx = nx if experts % nx == 0 else 1
    return jax.shard_map(
        functools.partial(shards, experts // nx, nx),
        mesh=mesh,
        in_specs=(
            P(("expert", "dp"), None),
            P(("expert", "dp"), None),
            P(("expert", "dp"), None),
            P("expert", None, None),
            P("expert", None, None),
            P("expert", None, None),
            P("expert", None, None),
            P("expert", None, None),
            P(),
        ),
        out_specs=(P("expert", "dp", None), P("expert", "dp", None), P(("expert", "dp"), None)),
        check_vma=False,
    )
```
